32 devices in a mesh: groups: 2 (over x), corpus: 8 (over z, y), replica: 2 (over core).
Axes of the slice: x: 2, y: 2, z: 4, core: 2. Of those that a mesh axis runs over, the one named last changes fastest.
Arguments:
- queries: bfloat16 [2048, 1024], P(('groups', 'corpus', 'replica')), parts along dimension 0, may hold values from -6 to 6
- codebook: bfloat16 [32, 1024], P('groups'), parts along dimension 0, may hold values from -0.1875 to 0.1875
- pq_codes: int32 [32768, 256], P(('groups', 'corpus')), parts along dimension 0, may hold values from 0 to 15
- full_rows: bfloat16 [32768, 1024], P(('groups', 'corpus')), parts along dimension 0, may hold values from -0.1875 to 0.1875
- probe_ids: int32 [16, 2, 8, 4], P('groups', 'replica', 'corpus'), parts along dimension 0, may hold values from 0 to 7, as said below
- probe_len: int32 [16, 2, 8], P('groups', 'replica', 'corpus'), parts along dimension 0, may hold values from 1 to 4, 16 in all within a row
- cand_shard: int32 [2048, 4, 4], P(('groups', 'corpus', 'replica')), parts along dimension 0, may hold values from 0 to 7, all different within a row; in each aligned block of 256 rows (0 to 255, 256 to 511, ..., all dimensions but the last counted through in order) at most 256 rows name the same one
- cand_row: int32 [2048, 4, 4], P(('groups', 'corpus', 'replica')), parts along dimension 0, may hold values from 0 to 2047
Outputs:
- approx_scores: bfloat16 [16, 2, 8, 4, 64, 256], P('groups', 'replica', 'corpus'), parts along dimension 0
- exact_scores: float32 [2048, 4, 4], P(('groups', 'corpus', 'replica')), parts along dimension 0
The draws below stay inside these ranges and needn't reach their ends.
There are 2 independent parts, one for each index of `groups`. The reference program is written for one: setup_inputs(seed, part) draws one part's arguments, and reference() takes and returns one part's arrays. A program takes and returns all parts, laid end to end along the dimension named above; each array names one. Nothing has to cross between parts.
Inputs may be any that keep to these rules, and one draw needn't show every extreme that they name: `probe_ids`: each list names 4 different posting blocks of the shard. `cand_shard`: the 4 candidates of a group lie on different shards; among the candidates of one query block at most 256 lie on any one shard, and some shard holds exactly 256 of them.
All inputs are finite; a program needn't handle non-finite values. No bound on the sum of `probe_len` on one device may be relied on, other than what follows from the above.
Results may differ from the reference program's by a relative error of at most 0.001.
Values may be sent and summed in bfloat16 or wider, within the bound.
No kernel may reach another device: no remote copies, remote signals or barrier semaphores. Data moves between devices by JAX's collectives and lax.ppermute only.
A program may use at most 128 MiB of HBM per device.

```python
import math
import jax
import jax.numpy as jnp
import numpy as np
from jax import lax

D = 1024
SUB = 4
M = 256
K = 16
B = 256
PB_SH = 8
R = 2048
NROWS = 16384
P_SIZE = 4
Q_DEV = 64
Q = 1024
CG = 4
TOPC = 4
CAP = 256
N_CORPUS = 8
N_REPLICA = 2


def draw_probe_ids(key, part):
    key = jax.random.fold_in(key, 11)
    random_keys = jax.random.randint(key, (N_CORPUS, N_REPLICA, N_CORPUS, PB_SH), 0, 1 << 20)
    ranked = random_keys * PB_SH + jnp.arange(PB_SH, dtype=jnp.int32)
    ordering = jnp.argsort(ranked, axis=-1)
    return ordering[..., :P_SIZE].astype(jnp.int32)


def with_ends(entries, own_key, smallest, high):
    index_at = [jax.random.randint(jax.random.fold_in(own_key, axis), (), 0, length) for axis, length in enumerate(entries.shape)]
    longest = entries.shape.index(max(entries.shape))
    next_to = index_at[:longest] + [(index_at[longest] + 1) % entries.shape[longest]] + index_at[longest + 1:]
    return entries.at[tuple(index_at)].set(smallest).at[tuple(next_to)].set(high)


def block_scale(key, dims, pieces, smallest, top_value):
    loudness = 1.0
    for axis_at, blocks in pieces:
        draws = jax.random.uniform(jax.random.fold_in(jax.random.fold_in(key, 6), axis_at), (blocks,), jnp.float32, smallest / len(pieces), top_value / len(pieces))
        loudness = loudness * jnp.repeat(jnp.exp(draws), dims[axis_at] // blocks).reshape((-1,) + (1,) * (len(dims) - 1 - axis_at))
    return loudness


def length_profile(amount, total, limit, lean):
    weights = [(1 << 20) // math.isqrt(standing ** lean) + 1 for standing in range(2, amount + 1)]
    surplus, holding = total - limit - (amount - 1), [1] * (amount - 1)
    while surplus > 0:
        candidates = [i for i in range(amount - 1) if holding[i] < limit]
        mass, remaining = sum([weights[i] for i in candidates]), surplus
        for i in candidates:
            addition = min(limit - holding[i], max(1, remaining * weights[i] // mass), surplus)
            holding[i] = holding[i] + addition
            surplus = surplus - addition
    return np.array([limit] + holding)


def ragged(own_key, number_of, total, limit, slope):
    if number_of == 2:
        one = jax.random.randint(own_key, (), max(1, total - limit), min(limit, total - 1) + 1)
        return jnp.stack([one, total - one])
    tallies = jnp.asarray(length_profile(number_of, total, limit, slope), jnp.int32)
    twos = (number_of - 1) // 2
    donor, taker = tallies[1:1 + 2 * twos:2], tallies[2:2 + 2 * twos:2]
    margin = jnp.minimum(donor - 1, limit - taker)
    shifted = jax.random.randint(jax.random.fold_in(own_key, 1), (twos,), 0, 1 << 20) % (margin + 1)
    tallies = tallies.at[1:1 + 2 * twos:2].set(donor - shifted).at[2:2 + 2 * twos:2].set(taker + shifted)
    return tallies[jax.random.permutation(jax.random.fold_in(own_key, 2), number_of)]


def routed_block(stream_key, own, number, rows, number_of, top, bound, lean):
    ranking = jax.random.permutation(stream_key, number_of)
    packed, usual = shares(number_of, rows * top, bound, lean, True), shares(number_of, rows * top, bound, lean, False)
    places = jnp.arange(number_of)

    def named(tallies, rotation):
        used = int((tallies > 0).sum())
        fixed = max(1, used // 4)
        shifted = fixed + (places - fixed + rotation * (used - fixed)) % max(1, number_of - fixed)
        return jnp.zeros((number_of,), jnp.int32).at[ranking[jnp.where(places < fixed, places, shifted)]].set(jnp.asarray(tallies, jnp.int32))

    tallies = jnp.where(number % 4 == 0, named(packed, number // 4), named(usual, number - number // 4 - 1))
    mixed = jax.random.permutation(jax.random.fold_in(own, 3), number_of)
    source_of, sink = mixed[0:number_of // 2 * 2:2], mixed[1:number_of // 2 * 2:2]
    margin = jnp.minimum(tallies[source_of] - 1, bound - tallies[sink]) // 2
    margin = jnp.where((source_of == ranking[0]) | (sink == ranking[0]) | (tallies[sink] == 0), 0, jnp.maximum(margin, 0))
    shifted = jax.random.randint(jax.random.fold_in(own, 4), (number_of // 2,), 0, 1 << 20) % (margin + 1)
    tallies = tallies.at[source_of].add(-shifted).at[sink].add(shifted)
    items = jnp.searchsorted(jnp.cumsum(tallies), jnp.arange(rows * top), side="right").astype(jnp.int32)
    grid = items.reshape(top, rows).T
    grid = grid[jax.random.permutation(jax.random.fold_in(own, 1), rows)]
    rotation = jax.random.randint(jax.random.fold_in(own, 2), (rows, 1), 0, top)
    return jnp.take_along_axis(grid, (jnp.arange(top)[None, :] + rotation) % top, axis=1)


def shares(amount, total, most, slope, full):
    loads = [(1 << 20) // math.isqrt(standing ** slope) + 1 for standing in range(1, amount + 1)]
    largest = most if full else min(most, max(-(-total // amount), total * loads[0] // sum(loads)))
    least = 1 if total - largest >= amount - 1 else 0
    holding, spare = [largest] + [least] * (amount - 1), total - largest - least * (amount - 1)
    while spare > 0:
        free = [i for i in range(1, amount) if holding[i] < largest] or [i for i in range(1, amount) if holding[i] < most]
        mass, budget = sum([loads[i] for i in free]), spare
        for i in free:
            more = min(most - holding[i], max(1, budget * loads[i] // mass), spare)
            holding[i] = holding[i] + more
            spare = spare - more
    return np.array(holding)


def scatter_about(key, shape, spread, most, shards=(), kind=jnp.bfloat16):
    drawn = jax.random.normal(key, shape, jnp.float32) * spread
    if len(shards) > 0:
        drawn = block_scale(key, shape, shards, -0.22, 0.18) * drawn
    return jnp.clip(drawn, min=-most, max=most).astype(kind)


def setup_inputs(seed: int = 0, part: int = 0) -> dict:
    key_of = jax.random.split(jax.random.key(seed), 9)
    own_keys = jax.random.split(jax.random.fold_in(key_of[8], part), 9)
    queries = scatter_about(own_keys[0], (Q, D), 1.0, 6.0, ((0, 16),))
    codebook = scatter_about(own_keys[1], (K, D), D ** -0.5, 0.1875)
    pq_codes = with_ends(jax.random.randint(own_keys[2], (NROWS, M), 0, K), jax.random.fold_in(own_keys[2], 1), 0, K - 1).astype(jnp.int32)
    full_rows = scatter_about(own_keys[3], (NROWS, D), D ** -0.5, 0.1875, ((0, 8),))
    probe_ids = draw_probe_ids(jax.random.fold_in(jax.random.fold_in(key_of[8], part), 71), part)
    probe_len = jax.vmap(lambda own: ragged(own, N_CORPUS, N_CORPUS * P_SIZE // 2, P_SIZE, 2))(jax.random.split(own_keys[5], N_CORPUS * N_REPLICA)).reshape((N_CORPUS, N_REPLICA, N_CORPUS)).astype(jnp.int32)
    cand_shard_keys = jax.random.split(jax.random.fold_in(own_keys[6], 1), Q * CG // (Q_DEV * CG))
    cand_shard_turns = jax.random.permutation(jax.random.fold_in(own_keys[6], 3), Q * CG // (Q_DEV * CG))
    cand_shard = jax.vmap(lambda own, number: routed_block(jax.random.fold_in(own_keys[6], 2), own, number, Q_DEV * CG, N_CORPUS, TOPC, CAP, 2))(cand_shard_keys, cand_shard_turns).reshape((Q, CG, TOPC))
    cand_row = with_ends(jax.random.randint(own_keys[7], (Q, CG, TOPC), 0, R), jax.random.fold_in(own_keys[7], 1), 0, R - 1).astype(jnp.int32)
    return {"queries": queries, "codebook": codebook, "pq_codes": pq_codes, "full_rows": full_rows, "probe_ids": probe_ids, "probe_len": probe_len, "cand_shard": cand_shard, "cand_row": cand_row}


def reference(queries, codebook, pq_codes, full_rows, probe_ids, probe_len, cand_shard, cand_row):
    block_count = N_CORPUS * N_REPLICA
    probe_table = probe_ids.reshape(block_count, N_CORPUS, P_SIZE)
    length_table = probe_len.reshape(block_count, N_CORPUS)
    slot_numbers = jnp.arange(P_SIZE, dtype=jnp.int32)[None, :]

    def one_shard(shard_index):
        shard_codes = lax.dynamic_slice_in_dim(pq_codes, shard_index * R, R, 0)
        widened = jnp.repeat(shard_codes, SUB, axis=1)
        decoded = jnp.take_along_axis(codebook, widened, axis=0)
        scores = jnp.dot(queries, decoded.T, preferred_element_type=jnp.float32)
        scores = scores.reshape(block_count, Q_DEV, PB_SH, B)
        chosen = jnp.take(probe_table, shard_index, axis=1)
        lengths = jnp.take(length_table, shard_index, axis=1)
        picked = jax.vmap(lambda block_scores, block_ids: jnp.take(block_scores, block_ids, axis=1))(scores, chosen)
        picked = jnp.transpose(picked, (0, 2, 1, 3))
        live_mask = slot_numbers < lengths[:, None]
        return jnp.where(live_mask[:, :, None, None], picked, 0.0).astype(jnp.bfloat16)

    per_shard = lax.map(one_shard, jnp.arange(N_CORPUS, dtype=jnp.int32))
    approx_scores = jnp.transpose(per_shard, (1, 0, 2, 3, 4)).reshape(N_CORPUS, N_REPLICA, N_CORPUS, P_SIZE, Q_DEV, B)

    flat_index = (cand_shard * R + cand_row).astype(jnp.int32)
    by_group = jnp.transpose(flat_index, (1, 0, 2))
    query_wide = queries.astype(jnp.float32)

    def one_group(group_index):
        fetched = jnp.take(full_rows, group_index, axis=0).astype(jnp.float32)
        return jnp.einsum("qtd,qd->qt", fetched, query_wide, precision=lax.Precision.HIGHEST)

    exact_scores = jnp.transpose(lax.map(one_group, by_group), (1, 0, 2))
    return approx_scores, exact_scores
```

```python
import functools

import jax
import jax.numpy as jnp
from jax import lax
from jax.experimental import pallas as pl
from jax.experimental.pallas import tpu as pltpu
from jax.sharding import PartitionSpec as P

B = 256
NT = (((1,), (1,)), ((), ()))
IN_VMEM = pl.BlockSpec(memory_space=pltpu.VMEM)
IN_SMEM = pl.BlockSpec(memory_space=pltpu.SMEM)
LIMIT = 24 * 2**20


def params():
    return pltpu.CompilerParams(vmem_limit_bytes=LIMIT)


def pick(table, index):
    return jnp.take_along_axis(table, index, axis=0, mode="promise_in_bounds")


def decode_kernel(codes_ref, book_ref, out_ref, expand_ref, *, sub_width, step):
    rows, code_count = codes_ref.shape
    features = book_ref.shape[1]
    owner = lax.broadcasted_iota(jnp.int32, (code_count, features), 1) // sub_width
    place = lax.broadcasted_iota(jnp.int32, (code_count, features), 0)
    expand_ref[...] = (owner == place).astype(jnp.bfloat16)

    @pl.loop(0, rows // step)
    def _(at):
        here = pl.ds(pl.multiple_of(at * step, step), step)
        codes = codes_ref[here, :].astype(jnp.bfloat16)
        for left in range(0, features, 128):
            lanes = slice(left, left + 128)
            if left % 256 == 0:
                wide = jnp.dot(
                    codes, expand_ref[:, left : left + 256], preferred_element_type=jnp.float32
                ).astype(jnp.int32)
            centroids = book_ref[:, lanes].astype(jnp.float32)
            low, high = centroids[:8], centroids[8:]
            pieces = []
            for top in range(0, step, 8):
                index = wide[top : top + 8, left % 256 : left % 256 + 128]
                inner = index & 7
                pieces.append(jnp.where(index >= 8, pick(high, inner), pick(low, inner)))
            out_ref[here, lanes] = jnp.concatenate(pieces, axis=0).astype(jnp.bfloat16)


def decode(pq_codes, codebook):
    rows, code_count = pq_codes.shape
    features = codebook.shape[1]
    return pl.pallas_call(
        functools.partial(decode_kernel, sub_width=features // code_count, step=256),
        out_shape=jax.ShapeDtypeStruct((rows, features), jnp.bfloat16),
        in_specs=[IN_VMEM, IN_VMEM],
        out_specs=IN_VMEM,
        scratch_shapes=[pltpu.VMEM((code_count, features), jnp.bfloat16)],
        compiler_params=params(),
        cost_estimate=pl.CostEstimate(
            flops=2 * rows * code_count * features, bytes_accessed=8 * 2**20, transcendentals=0
        ),
        name="decode",
    )(pq_codes, codebook)


def exact_kernel(base_ref, cand_ref, rows_ref, *refs, places, groups):
    blocks, outs, stack = refs[: len(places)], refs[len(places) : -1], refs[-1]
    query_rows = blocks[0].shape[0]
    row_count = rows_ref.shape[0]
    per_query = cand_ref.shape[0]
    tops = per_query // groups
    for at, block in enumerate(blocks):
        stack[at * query_rows : (at + 1) * query_rows, :] = block[...]
    width = len(blocks) * query_rows
    scores = lax.dot_general(
        rows_ref[...], stack[...], NT, preferred_element_type=jnp.float32
    )
    wanted = (
        jnp.concatenate(
            [cand_ref[:, p * query_rows : (p + 1) * query_rows] for p in places], axis=1
        )
        - base_ref[0]
    )
    mine = (wanted >= 0) & (wanted < row_count)
    kept = jnp.where(mine, wanted, -1)
    down = lax.broadcasted_iota(jnp.int32, (8, width), 0)
    found = []
    for group in range(groups):
        row = jnp.max(kept[group * tops : (group + 1) * tops], axis=0, keepdims=True)
        row = jnp.broadcast_to(row, (8, width)) - down
        total = jnp.zeros((8, width), jnp.float32)
        for top in range(0, row_count, 8):
            total = jnp.where(row == top, scores[top : top + 8], total)
        total = jnp.sum(total, axis=0, keepdims=True)
        found.append(jnp.broadcast_to(total, (tops, width)))
    answer = jnp.where(mine, jnp.concatenate(found, axis=0), 0.0)
    for at, out in enumerate(outs):
        out[...] = answer[:, at * query_rows : (at + 1) * query_rows]


def exact(base, cands, full_rows, blocks, places, groups):
    query_rows, features = blocks[0].shape
    per_query = cands.shape[0]
    count = len(blocks)
    return pl.pallas_call(
        functools.partial(exact_kernel, places=places, groups=groups),
        out_shape=[jax.ShapeDtypeStruct((per_query, query_rows), jnp.float32)] * count,
        in_specs=[IN_SMEM] + [IN_VMEM] * (2 + count),
        out_specs=[IN_VMEM] * count,
        scratch_shapes=[pltpu.VMEM((count * query_rows, features), jnp.bfloat16)],
        compiler_params=params(),
        cost_estimate=pl.CostEstimate(
            flops=2 * count * query_rows * features * full_rows.shape[0],
            bytes_accessed=4 * 2**20,
            transcendentals=0,
        ),
        name="exact",
    )(base, cands, full_rows, *blocks)


def approx_kernel(where_ref, ids_ref, len_ref, rows_ref, *refs):
    blocks, out_ref, stack, scores = refs[:-3], refs[-3], refs[-2], refs[-1]
    query_rows = blocks[0].shape[0]
    slots = out_ref.shape[1]
    for at, block in enumerate(blocks):
        stack[at * query_rows : (at + 1) * query_rows, :] = block[...]
    for block in range(scores.shape[0]):
        scores[block] = lax.dot_general(
            stack[...],
            rows_ref[block * B : (block + 1) * B, :],
            NT,
            preferred_element_type=jnp.float32,
        ).astype(jnp.bfloat16)

    for at in range(len(blocks)):
        owner = where_ref[at]
        here = slice(at * query_rows, (at + 1) * query_rows)
        for slot in range(slots):
            picked = scores[ids_ref[owner, slot], here, :]
            out_ref[owner, slot] = jnp.where(slot < len_ref[owner], picked, jnp.zeros_like(picked))


def approx(where, probe_ids, probe_len, decoded, blocks):
    query_rows, features = blocks[0].shape
    count = len(blocks)
    slots = probe_ids.shape[1]
    block_count = decoded.shape[0] // B
    width = count * query_rows
    return pl.pallas_call(
        approx_kernel,
        out_shape=jax.ShapeDtypeStruct((count, slots, query_rows, B), jnp.bfloat16),
        in_specs=[IN_SMEM] * 3 + [IN_VMEM] * (1 + count),
        out_specs=IN_VMEM,
        scratch_shapes=[
            pltpu.VMEM((width, features), jnp.bfloat16),
            pltpu.VMEM((block_count, width, B), jnp.bfloat16),
        ],
        compiler_params=params(),
        cost_estimate=pl.CostEstimate(
            flops=2 * width * features * decoded.shape[0],
            bytes_accessed=4 * 2**20,
            transcendentals=0,
        ),
        name="approx",
    )(where, probe_ids, probe_len, decoded, *blocks)


def swap(x, distance, shards):
    return lax.ppermute(x, "corpus", [(i, i ^ distance) for i in range(shards)])


def local(queries, codebook, pq_codes, full_rows, probe_ids, probe_len, cand_shard, cand_row):
    shards = lax.axis_size("corpus")
    me = lax.axis_index("corpus")
    query_rows, features = queries.shape
    slab_rows = full_rows.shape[0]
    groups, tops = cand_shard.shape[1:]
    per_query = groups * tops
    slots = probe_ids.shape[-1]
    base = (me * slab_rows).astype(jnp.int32).reshape(1)
    ids = probe_ids.reshape(shards, slots)
    lens = probe_len.reshape(shards)
    wanted = (cand_shard * slab_rows + cand_row).reshape(query_rows, per_query).T

    if shards == 8:
        far = swap(queries, 4, shards)
        near = swap(queries, 2, shards)
        side = swap(queries, 1, shards)
        cross = swap(queries, 7, shards)
        near_side = swap(near, 1, shards)
        far_near = swap(far, 2, shards)
        far_side = swap(far, 1, shards)
        blocks = [queries, side, near, near_side, far, far_side, far_near, cross]
        for distance in (1, 2, 4):
            wanted = jnp.concatenate([wanted, swap(wanted, distance, shards)], axis=1)
        decoded = decode(pq_codes, codebook)
        places = list(range(8))
        answers = exact(base, wanted, full_rows, blocks, places, groups)
        back = [answers[0]] + [swap(answers[p], p, shards) for p in places[1:]]
        where = me ^ jnp.arange(8, dtype=jnp.int32)
        approx_scores = approx(where, ids, lens, decoded, blocks)
        total = functools.reduce(jnp.add, back)
    else:
        gathered = lax.all_gather(queries, "corpus", axis=0)
        asked = lax.all_gather(wanted, "corpus", axis=0)
        decoded = decode(pq_codes, codebook)
        answers, pieces = [], []
        step = 4
        for first in range(0, shards, step):
            picked = list(range(first, first + step))
            cands = jnp.concatenate([asked[p] for p in picked], axis=1)
            answers += exact(
                base, cands, full_rows, [gathered[p] for p in picked], list(range(step)), groups
            )
            pieces.append(
                approx(
                    jnp.arange(step, dtype=jnp.int32),
                    ids[first : first + step],
                    lens[first : first + step],
                    decoded,
                    [gathered[p] for p in picked],
                )
            )
        approx_scores = jnp.concatenate(pieces, axis=0)
        back = lax.all_to_all(jnp.stack(answers), "corpus", 0, 0, tiled=True)
        total = jnp.sum(back, axis=0)

    approx_scores = approx_scores.reshape(shards, 1, 1, slots, query_rows, B)
    return approx_scores, total.T.reshape(query_rows, groups, tops)


def solution(mesh):
    return jax.shard_map(
        local,
        mesh=mesh,
        in_specs=(
            P(("groups", "corpus", "replica"), None),
            P("groups", None),
            P(("groups", "corpus"), None),
            P(("groups", "corpus"), None),
            P("groups", "replica", "corpus", None),
            P("groups", "replica", "corpus"),
            P(("groups", "corpus", "replica"), None, None),
            P(("groups", "corpus", "replica"), None, None),
        ),
        out_specs=(
            P("groups", "replica", "corpus", None, None, None),
            P(("groups", "corpus", "replica"), None, None),
        ),
        check_vma=False,
    )
```

```python
import functools

import jax
import jax.numpy as jnp
from jax import lax
from jax.experimental import pallas as pl
from jax.experimental.pallas import tpu as pltpu
from jax.sharding import PartitionSpec as P

B = 256
NT = (((1,), (1,)), ((), ()))
IN_VMEM = pl.BlockSpec(memory_space=pltpu.VMEM)
IN_HBM = pl.BlockSpec(memory_space=pl.ANY)
IN_SMEM = pl.BlockSpec(memory_space=pltpu.SMEM)
LIMIT = 24 * 2**20


def params():
    return pltpu.CompilerParams(vmem_limit_bytes=LIMIT)


def pick(table, index):
    return jnp.take_along_axis(table, index, axis=0, mode="promise_in_bounds")


def regroup_matrix(sub_width):
    run = 256 // sub_width
    source = lax.broadcasted_iota(jnp.int32, (256, 256), 0)
    target = lax.broadcasted_iota(jnp.int32, (256, 256), 1)
    return (source == (target % run) * sub_width + target // run).astype(jnp.bfloat16)


def decode_kernel(
    queries_ref, codes_ref, book_ref, rows_ref, shard_ref, row_ref,
    out_ref, rows_out, queries_out, wanted_out,
    codes, book, tables, shard, row, code_sems, row_sems, small_sems,
    *, step,
):
    row_count, code_count = codes_ref.shape
    features = book_ref.shape[1]
    sub_width = features // code_count
    parts = row_count // step
    small = [
        pltpu.make_async_copy(source, target, small_sems.at[at])
        for at, (source, target) in enumerate(
            [(book_ref, book), (shard_ref, shard), (row_ref, row), (queries_ref, queries_out)]
        )
    ]
    for copy in small:
        copy.start()
    for part in range(parts):
        here = pl.ds(part * step, step)
        pltpu.make_async_copy(codes_ref.at[here], codes.at[here], code_sems.at[part]).start()
    row_copies = []
    for part in range(4):
        here = pl.ds(part * (row_count // 4), row_count // 4)
        row_copies.append(
            pltpu.make_async_copy(rows_ref.at[here], rows_out.at[here], row_sems.at[part])
        )
        row_copies[-1].start()
    regroup = regroup_matrix(sub_width)
    small[0].wait()
    for left in range(0, features, 256):
        tables[:, left : left + 256] = jnp.dot(
            book[:, left : left + 256], regroup, preferred_element_type=jnp.float32
        )

    @pl.loop(0, parts)
    def _(at):
        start = pl.multiple_of(at * step, step)
        here = pl.ds(start, step)
        pltpu.make_async_copy(codes_ref.at[here], codes.at[here], code_sems.at[at]).wait()
        first = lax.broadcasted_iota(jnp.int32, (step, 128), 1) < 64
        for pair in range(code_count // 128):
            both = codes[here, pair * 128 : (pair + 1) * 128]
            turned = pltpu.roll(both, 64, 1)
            for side in range(2):
                index = jnp.where(first, both, turned) if side == 0 else jnp.where(first, turned, both)
                inner = index & 7
                upper = index >= 8
                for half in range(2):
                    left = (pair * 2 + side) * 256 + half * 128
                    low = tables[:8, left : left + 128]
                    high = tables[8:16, left : left + 128]
                    pieces = []
                    for top in range(0, step, 8):
                        near = slice(top, top + 8)
                        pieces.append(
                            jnp.where(upper[near], pick(high, inner[near]), pick(low, inner[near]))
                        )
                    out_ref[here, left : left + 128] = jnp.concatenate(pieces, axis=0).astype(
                        jnp.bfloat16
                    )

    for copy in small[1:]:
        copy.wait()
    wanted_out[...] = shard[...] * row_count + row[...]
    for copy in row_copies:
        copy.wait()


def decode(queries, pq_codes, codebook, full_rows, cand_shard, cand_row):
    rows, code_count = pq_codes.shape
    features = codebook.shape[1]
    step = 256
    return pl.pallas_call(
        functools.partial(decode_kernel, step=step),
        out_shape=[
            pltpu.VMEM((rows, features), jnp.bfloat16),
            pltpu.VMEM(full_rows.shape, full_rows.dtype),
            pltpu.VMEM(queries.shape, queries.dtype),
            pltpu.VMEM(cand_row.shape, jnp.int32),
        ],
        in_specs=[IN_HBM] * 6,
        out_specs=[IN_VMEM] * 4,
        scratch_shapes=[
            pltpu.VMEM(pq_codes.shape, jnp.int32),
            pltpu.VMEM(codebook.shape, codebook.dtype),
            pltpu.VMEM(codebook.shape, jnp.float32),
            pltpu.VMEM(cand_row.shape, jnp.int32),
            pltpu.VMEM(cand_row.shape, jnp.int32),
            pltpu.SemaphoreType.DMA((rows // step,)),
            pltpu.SemaphoreType.DMA((4,)),
            pltpu.SemaphoreType.DMA((4,)),
        ],
        compiler_params=params(),
        cost_estimate=pl.CostEstimate(
            flops=2 * rows * code_count * features, bytes_accessed=8 * 2**20, transcendentals=0
        ),
        name="decode",
    )(*map(in_hbm, (queries, pq_codes, codebook, full_rows, cand_shard, cand_row)))


def in_hbm(x):
    return pltpu.with_memory_space_constraint(x, pltpu.HBM)


def in_vmem(x):
    return pltpu.with_memory_space_constraint(x, pltpu.VMEM)


def exact_kernel(cand_ref, rows_ref, *refs, groups):
    blocks, out_ref, stack = refs[:-2], refs[-2], refs[-1]
    query_rows = blocks[0].shape[0]
    row_count = rows_ref.shape[0]
    per_query, width = cand_ref.shape
    tops = per_query // groups
    for at, block in enumerate(blocks):
        stack[at * query_rows : (at + 1) * query_rows, :] = block[...]
    scores = lax.dot_general(
        rows_ref[...], stack[...], NT, preferred_element_type=jnp.float32
    )
    wanted = cand_ref[...] - lax.axis_index("corpus") * row_count
    mine = (wanted >= 0) & (wanted < row_count)
    kept = jnp.where(mine, wanted, -1)
    down = lax.broadcasted_iota(jnp.int32, (8, width), 0)
    found = []
    for group in range(groups):
        row = jnp.max(kept[group * tops : (group + 1) * tops], axis=0, keepdims=True)
        row = jnp.broadcast_to(row, (8, width)) - down
        total = jnp.zeros((8, width), jnp.float32)
        for top in range(0, row_count, 8):
            total = jnp.where(row == top, scores[top : top + 8], total)
        total = jnp.sum(total, axis=0, keepdims=True)
        found.append(jnp.broadcast_to(total, (tops, width)))
    out_ref[...] = jnp.where(mine, jnp.concatenate(found, axis=0), 0.0)


def exact(cands, full_rows, blocks, groups):
    query_rows, features = blocks[0].shape
    count = len(blocks)
    return pl.pallas_call(
        functools.partial(exact_kernel, groups=groups),
        out_shape=jax.ShapeDtypeStruct(cands.shape, jnp.float32),
        in_specs=[IN_VMEM] * (2 + count),
        out_specs=IN_VMEM,
        scratch_shapes=[pltpu.VMEM((count * query_rows, features), jnp.bfloat16)],
        compiler_params=params(),
        cost_estimate=pl.CostEstimate(
            flops=2 * count * query_rows * features * full_rows.shape[0],
            bytes_accessed=4 * 2**20,
            transcendentals=0,
        ),
        name="exact",
    )(cands, in_vmem(full_rows), *map(in_vmem, blocks))


def scores_kernel(rows_ref, *refs, sub_width):
    blocks, out_ref, stack = refs[:-2], refs[-2], refs[-1]
    query_rows, features = blocks[0].shape
    regroup = regroup_matrix(sub_width)
    for at, block in enumerate(blocks):
        stack[at * query_rows : (at + 1) * query_rows, :] = block[...]
    for left in range(0, features, 256):
        run = slice(left, left + 256)
        stack[:, run] = jnp.dot(
            stack[:, run], regroup, preferred_element_type=jnp.float32
        ).astype(jnp.bfloat16)
    for block in range(out_ref.shape[0]):
        out_ref[block] = lax.dot_general(
            stack[...],
            rows_ref[block * B : (block + 1) * B, :],
            NT,
            preferred_element_type=jnp.float32,
        ).astype(jnp.bfloat16)


def score_blocks(decoded, blocks, sub_width):
    query_rows, features = blocks[0].shape
    width = len(blocks) * query_rows
    block_count = decoded.shape[0] // B
    return pl.pallas_call(
        functools.partial(scores_kernel, sub_width=sub_width),
        out_shape=pltpu.VMEM((block_count, width, B), jnp.bfloat16),
        in_specs=[IN_VMEM] * (1 + len(blocks)),
        out_specs=IN_VMEM,
        scratch_shapes=[pltpu.VMEM((width, features), jnp.bfloat16)],
        compiler_params=params(),
        cost_estimate=pl.CostEstimate(
            flops=2 * width * features * decoded.shape[0],
            bytes_accessed=4 * 2**20,
            transcendentals=0,
        ),
        name="score_blocks",
    )(in_vmem(decoded), *map(in_vmem, blocks))


def choose_kernel(ids_ref, len_ref, scores_ref, out_ref, *, mirrored):
    count, slots, query_rows, _ = out_ref.shape
    for at in range(count):
        owner = lax.axis_index("corpus") ^ at if mirrored else at
        here = slice(at * query_rows, (at + 1) * query_rows)
        for slot in range(slots):
            picked = scores_ref[ids_ref[slot, owner], here, :]
            out_ref[owner, slot] = jnp.where(slot < len_ref[owner], picked, jnp.zeros_like(picked))


def choose(probe_ids, probe_len, scores, mirrored):
    slots, count = probe_ids.shape
    query_rows = scores.shape[1] // count
    return pl.pallas_call(
        functools.partial(choose_kernel, mirrored=mirrored),
        out_shape=jax.ShapeDtypeStruct((count, slots, query_rows, B), jnp.bfloat16),
        in_specs=[IN_SMEM] * 2 + [IN_VMEM],
        out_specs=IN_VMEM,
        compiler_params=params(),
        cost_estimate=pl.CostEstimate(flops=0, bytes_accessed=4 * 2**20, transcendentals=0),
        name="choose",
    )(probe_ids, probe_len, in_vmem(scores))


def swap(x, distance, shards):
    return lax.ppermute(x, "corpus", [(i, i ^ distance) for i in range(shards)])


def local(queries, codebook, pq_codes, full_rows, probe_ids, probe_len, cand_shard, cand_row):
    shards = lax.axis_size("corpus")
    query_rows, features = queries.shape
    groups, tops = cand_shard.shape[1:]
    per_query = groups * tops
    slots = probe_ids.shape[-1]
    sub_width = features // pq_codes.shape[1]
    ids = probe_ids.reshape(shards, slots).T
    lens = probe_len.reshape(shards)
    prepare = functools.partial(
        decode,
        queries,
        pq_codes,
        codebook,
        full_rows,
        cand_shard.reshape(query_rows, per_query).T,
        cand_row.reshape(query_rows, per_query).T,
    )

    if shards == 8:
        far = swap(queries, 4, shards)
        near = swap(queries, 2, shards)
        side = swap(queries, 1, shards)
        decoded, rows, own, wanted = prepare()
        cross = swap(own, 7, shards)
        near_side = swap(near, 1, shards)
        far_near = swap(far, 2, shards)
        far_side = swap(far, 1, shards)
        for distance in (1, 2):
            wanted = jnp.concatenate([wanted, swap(wanted, distance, shards)], axis=1)
        wanted_far = swap(wanted, 4, shards)
        this_half = [own, side, near, near_side]
        that_half = [far, far_side, far_near, cross]
        kept = exact(wanted, rows, this_half, groups)
        sent = exact(wanted_far, rows, that_half, groups)
        scores = score_blocks(decoded, this_half + that_half, sub_width)
        approx_scores = choose(ids, lens, scores, True)
        for distance in (4, 2, 1):
            kept = kept + swap(sent, distance, shards)
            half = kept.shape[1] // 2
            kept, sent = kept[:, :half], kept[:, half:]
        total = jnp.concatenate([kept, sent], axis=1)
    else:
        gathered = lax.all_gather(queries, "corpus", axis=0)
        decoded, rows, _, wanted = prepare()
        asked = lax.all_gather(wanted, "corpus", axis=0)
        answers, pieces = [], []
        step = 4
        for first in range(0, shards, step):
            picked = list(range(first, first + step))
            blocks = [gathered[p] for p in picked]
            cands = jnp.concatenate([asked[p] for p in picked], axis=1)
            found = exact(cands, rows, blocks, groups)
            answers += [found[:, p * query_rows : (p + 1) * query_rows] for p in range(step)]
            scores = score_blocks(decoded, blocks, sub_width)
            some = slice(first, first + step)
            pieces.append(choose(ids[:, some], lens[some], scores, False))
        approx_scores = jnp.concatenate(pieces, axis=0)
        back = lax.all_to_all(jnp.stack(answers), "corpus", 0, 0, tiled=True)
        total = jnp.sum(back, axis=0)

    approx_scores = approx_scores.reshape(shards, 1, 1, slots, query_rows, B)
    return approx_scores, total.T.reshape(query_rows, groups, tops)


def solution(mesh):
    return jax.shard_map(
        local,
        mesh=mesh,
        in_specs=(
            P(("groups", "corpus", "replica"), None),
            P("groups", None),
            P(("groups", "corpus"), None),
            P(("groups", "corpus"), None),
            P("groups", "replica", "corpus", None),
            P("groups", "replica", "corpus"),
            P(("groups", "corpus", "replica"), None, None),
            P(("groups", "corpus", "replica"), None, None),
        ),
        out_specs=(
            P("groups", "replica", "corpus", None, None, None),
            P(("groups", "corpus", "replica"), None, None),
        ),
        check_vma=False,
    )
```

```python
import functools

import jax
import jax.numpy as jnp
from jax import lax
from jax.experimental import pallas as pl
from jax.experimental.pallas import tpu as pltpu
from jax.sharding import PartitionSpec as P

B = 256
NT = (((1,), (1,)), ((), ()))
IN_VMEM = pl.BlockSpec(memory_space=pltpu.VMEM)
IN_HBM = pl.BlockSpec(memory_space=pl.ANY)
IN_SMEM = pl.BlockSpec(memory_space=pltpu.SMEM)
EXACT_COST = 0
LIMIT = 24 * 2**20


def params():
    return pltpu.CompilerParams(vmem_limit_bytes=LIMIT)


def pick(table, index):
    return jnp.take_along_axis(table, index, axis=0, mode="promise_in_bounds")


def regroup_matrix(sub_width):
    run = 256 // sub_width
    source = lax.broadcasted_iota(jnp.int32, (256, 256), 0)
    target = lax.broadcasted_iota(jnp.int32, (256, 256), 1)
    return (source == (target % run) * sub_width + target // run).astype(jnp.bfloat16)


def pack_kernel(
    queries_ref, shard_ref, row_ref, out_ref, shard, row, sems, *, row_count
):
    query_rows, features = queries_ref.shape
    strips = features // 128
    copies = [
        pltpu.make_async_copy(shard_ref, shard, sems.at[strips]),
        pltpu.make_async_copy(row_ref, row, sems.at[strips + 1]),
    ]
    for strip in range(strips):
        copies.append(
            pltpu.make_async_copy(
                queries_ref.at[:, pl.ds(strip * 128, 128)],
                out_ref.at[pl.ds(strip * query_rows, query_rows)],
                sems.at[strip],
            )
        )
    for copy in copies:
        copy.start()
    copies[0].wait()
    copies[1].wait()
    place = shard[...] * (row_count // B) + row[...] // B
    tail = jnp.concatenate([place, row[...] % B], axis=1)
    out_ref[strips * query_rows :, :] = tail.astype(jnp.float32).astype(jnp.bfloat16)
    for copy in copies[2:]:
        copy.wait()


def pack(queries, cand_shard, cand_row, row_count):
    query_rows, features = queries.shape
    per_query = cand_row.shape[0]
    strips = features // 128
    return pl.pallas_call(
        functools.partial(pack_kernel, row_count=row_count),
        out_shape=pltpu.VMEM((strips * query_rows + per_query, 128), jnp.bfloat16),
        in_specs=[IN_HBM] * 3,
        out_specs=IN_VMEM,
        scratch_shapes=[
            pltpu.VMEM(cand_row.shape, jnp.int32),
            pltpu.VMEM(cand_row.shape, jnp.int32),
            pltpu.SemaphoreType.DMA((strips + 2,)),
        ],
        compiler_params=params(),
        cost_estimate=cost(0),
        name="pack",
    )(*map(in_hbm, (queries, cand_shard, cand_row)))


def decode_kernel(
    codes_ref, book_ref, rows_ref, out_ref, rows_out, codes, book, tables, sems, row_sems, *, step
):
    row_count, features = out_ref.shape
    code_count = codes_ref.shape[1]
    parts = row_count // step

    def fetch(part):
        here = pl.ds(pl.multiple_of(part * step, step), step)
        return pltpu.make_async_copy(codes_ref.at[here], codes.at[here], sems.at[part])

    book_copy = pltpu.make_async_copy(book_ref, book, sems.at[parts])
    book_copy.start()
    for part in range(parts):
        fetch(part).start()
    row_copies = []
    piece = row_count // row_sems.shape[0]
    for at in range(row_sems.shape[0]):
        here = pl.ds(at * piece, piece)
        row_copies.append(
            pltpu.make_async_copy(rows_ref.at[here], rows_out.at[here], row_sems.at[at])
        )
        row_copies[-1].start()
    regroup = regroup_matrix(features // code_count)
    book_copy.wait()
    for left in range(0, features, 256):
        tables[:, left : left + 256] = jnp.dot(
            book[:, left : left + 256], regroup, preferred_element_type=jnp.float32
        )

    @pl.loop(0, parts)
    def _(at):
        fetch(at).wait()
        here = pl.ds(pl.multiple_of(at * step, step), step)
        first = lax.broadcasted_iota(jnp.int32, (step, 128), 1) < 64
        for pair in range(code_count // 128):
            both = codes[here, pair * 128 : (pair + 1) * 128]
            turned = pltpu.roll(both, 64, 1)
            for side in range(2):
                index = jnp.where(first, both, turned) if side == 0 else jnp.where(first, turned, both)
                inner = index & 7
                upper = index >= 8
                for half in range(2):
                    left = (pair * 2 + side) * 256 + half * 128
                    low = tables[:8, left : left + 128]
                    high = tables[8:16, left : left + 128]
                    pieces = []
                    for top in range(0, step, 8):
                        near = slice(top, top + 8)
                        pieces.append(
                            jnp.where(upper[near], pick(high, inner[near]), pick(low, inner[near]))
                        )
                    out_ref[here, left : left + 128] = jnp.concatenate(pieces, axis=0).astype(
                        jnp.bfloat16
                    )

    for copy in row_copies:
        copy.wait()


def decode(pq_codes, codebook, full_rows):
    features = codebook.shape[1]
    rows = pq_codes.shape[0]
    step = 256
    return pl.pallas_call(
        functools.partial(decode_kernel, step=step),
        out_shape=[
            pltpu.VMEM((rows, features), jnp.bfloat16),
            pltpu.VMEM(full_rows.shape, full_rows.dtype),
        ],
        in_specs=[IN_HBM] * 3,
        out_specs=[IN_VMEM] * 2,
        scratch_shapes=[
            pltpu.VMEM(pq_codes.shape, jnp.int32),
            pltpu.VMEM(codebook.shape, codebook.dtype),
            pltpu.VMEM(codebook.shape, jnp.float32),
            pltpu.SemaphoreType.DMA((rows // step + 1,)),
            pltpu.SemaphoreType.DMA((4,)),
        ],
        compiler_params=params(),
        cost_estimate=cost(0),
        name="decode",
    )(*map(in_hbm, (pq_codes, codebook, full_rows)))


def cost(size):
    return pl.CostEstimate(flops=size * 10**9, bytes_accessed=size * 2**20, transcendentals=0)


def in_hbm(x):
    return pltpu.with_memory_space_constraint(x, pltpu.HBM)


def in_vmem(x):
    return pltpu.with_memory_space_constraint(x, pltpu.VMEM)


def count_queries(block, rows, per_query):
    return (block.shape[0] - per_query) * 128 // rows.shape[1]


def fill(stack, blocks):
    query_rows = stack.shape[0] // len(blocks)
    for at, block in enumerate(blocks):
        for strip in range(stack.shape[1] // 128):
            stack[at * query_rows : (at + 1) * query_rows, strip * 128 : (strip + 1) * 128] = block[
                strip * query_rows : (strip + 1) * query_rows, :
            ]


def find(stack, rows_ref, blocks, per_query, groups):
    row_count = rows_ref.shape[0]
    width = stack.shape[0]
    query_rows = width // len(blocks)
    tops = per_query // groups
    scores = lax.dot_general(
        rows_ref[...], stack[...], NT, preferred_element_type=jnp.float32
    )
    tails = [block[-per_query:, :].astype(jnp.int32) for block in blocks]
    wanted = jnp.concatenate(
        [tail[:, :query_rows] * B + tail[:, query_rows : 2 * query_rows] for tail in tails], axis=1
    )
    wanted = wanted - lax.axis_index("corpus") * row_count
    mine = (wanted >= 0) & (wanted < row_count)
    kept = jnp.where(mine, wanted, -1)
    down = lax.broadcasted_iota(jnp.int32, (8, width), 0)
    found = []
    for group in range(groups):
        row = jnp.max(kept[group * tops : (group + 1) * tops], axis=0, keepdims=True)
        row = jnp.broadcast_to(row, (8, width)) - down
        total = jnp.zeros((8, width), jnp.float32)
        for top in range(0, row_count, 8):
            total = jnp.where(row == top, scores[top : top + 8], total)
        total = jnp.sum(total, axis=0, keepdims=True)
        found.append(jnp.broadcast_to(total, (tops, width)))
    return jnp.where(mine, jnp.concatenate(found, axis=0), 0.0)


def score(stack, decoded_ref, out_ref, sub_width):
    regroup = regroup_matrix(sub_width)
    for left in range(0, stack.shape[1], 256):
        run = slice(left, left + 256)
        stack[:, run] = jnp.dot(
            stack[:, run], regroup, preferred_element_type=jnp.float32
        ).astype(jnp.bfloat16)
    for block in range(out_ref.shape[0]):
        out_ref[block] = lax.dot_general(
            stack[...],
            decoded_ref[block * B : (block + 1) * B, :],
            NT,
            preferred_element_type=jnp.float32,
        ).astype(jnp.bfloat16)


def exact_kernel(rows_ref, *refs, per_query, groups):
    blocks, (found_ref, stack) = refs[:-2], refs[-2:]
    fill(stack, blocks)
    found_ref[...] = find(stack, rows_ref, blocks, per_query, groups)


def exact(full_rows, blocks, groups, tops):
    per_query = groups * tops
    width = len(blocks) * count_queries(blocks[0], full_rows, per_query)
    return pl.pallas_call(
        functools.partial(exact_kernel, per_query=per_query, groups=groups),
        out_shape=pltpu.VMEM((per_query, width), jnp.float32),
        in_specs=[IN_VMEM] * (1 + len(blocks)),
        out_specs=IN_VMEM,
        scratch_shapes=[pltpu.VMEM((width, full_rows.shape[1]), jnp.bfloat16)],
        compiler_params=params(),
        cost_estimate=cost(0),
        name="exact",
    )(*map(in_vmem, [full_rows] + blocks))


def scores_kernel(decoded_ref, *refs, sub_width):
    blocks, (scores_ref, stack) = refs[:-2], refs[-2:]
    fill(stack, blocks)
    score(stack, decoded_ref, scores_ref, sub_width)


def score_blocks(decoded, blocks, sub_width, per_query):
    width = len(blocks) * count_queries(blocks[0], decoded, per_query)
    rows, features = decoded.shape
    return pl.pallas_call(
        functools.partial(scores_kernel, sub_width=sub_width),
        out_shape=pltpu.VMEM((rows // B, width, B), jnp.bfloat16),
        in_specs=[IN_VMEM] * (1 + len(blocks)),
        out_specs=IN_VMEM,
        scratch_shapes=[pltpu.VMEM((width, features), jnp.bfloat16)],
        compiler_params=params(),
        cost_estimate=cost(0),
        name="score_blocks",
    )(*map(in_vmem, [decoded] + blocks))


def place_scores(ids_ref, len_ref, scores_ref, out_ref, owners):
    query_rows = out_ref.shape[2]
    for at, owner in enumerate(owners):
        here = slice(at * query_rows, (at + 1) * query_rows)
        for slot in range(out_ref.shape[1]):
            picked = scores_ref[ids_ref[slot, owner], here, :]
            out_ref[owner, slot] = jnp.where(slot < len_ref[owner], picked, jnp.zeros_like(picked))


def late_approx_kernel(
    ids_ref, len_ref, decoded_ref, scores_ref, *refs, places, sub_width
):
    blocks, (out_ref, stack, late_scores) = refs[:-3], refs[-3:]
    fill(stack, blocks)
    me = lax.axis_index("corpus")
    owners = [me ^ place for place in places]
    half = len(places) // 2
    place_scores(ids_ref, len_ref, scores_ref, out_ref, owners[:half])
    score(stack, decoded_ref, late_scores, sub_width)
    place_scores(ids_ref, len_ref, late_scores, out_ref, owners[half:])


def late_approx(probe_ids, probe_len, decoded, scores, blocks, places, sub_width):
    block_count, width, _ = scores.shape
    slots = probe_ids.shape[0]
    query_rows = width // len(blocks)
    return pl.pallas_call(
        functools.partial(late_approx_kernel, places=places, sub_width=sub_width),
        out_shape=pltpu.VMEM((len(places), slots, query_rows, B), jnp.bfloat16),
        in_specs=[IN_SMEM] * 2 + [IN_VMEM] * (2 + len(blocks)),
        out_specs=IN_VMEM,
        scratch_shapes=[
            pltpu.VMEM((width, decoded.shape[1]), jnp.bfloat16),
            pltpu.VMEM(scores.shape, jnp.bfloat16),
        ],
        compiler_params=params(),
        cost_estimate=cost(10),
        name="late_approx",
    )(probe_ids, probe_len, *map(in_vmem, [decoded, scores] + blocks))


def choose_kernel(ids_ref, len_ref, scores_ref, out_ref):
    place_scores(ids_ref, len_ref, scores_ref, out_ref, range(out_ref.shape[0]))


def choose(probe_ids, probe_len, scores):
    slots, count = probe_ids.shape
    query_rows = scores.shape[1] // count
    return pl.pallas_call(
        choose_kernel,
        out_shape=jax.ShapeDtypeStruct((count, slots, query_rows, B), jnp.bfloat16),
        in_specs=[IN_SMEM] * 2 + [IN_VMEM],
        out_specs=IN_VMEM,
        compiler_params=params(),
        name="choose",
    )(probe_ids, probe_len, scores)


def swap(x, distance, shards):
    return lax.ppermute(x, "corpus", [(i, i ^ distance) for i in range(shards)])


def local(queries, codebook, pq_codes, full_rows, probe_ids, probe_len, cand_shard, cand_row):
    shards = lax.axis_size("corpus")
    query_rows, features = queries.shape
    row_count = full_rows.shape[0]
    groups, tops = cand_shard.shape[1:]
    per_query = groups * tops
    slots = probe_ids.shape[-1]
    sub_width = features // pq_codes.shape[1]
    ids = probe_ids.reshape(shards, slots).T
    lens = probe_len.reshape(shards)
    own = pack(
        queries,
        cand_shard.reshape(query_rows, per_query).T,
        cand_row.reshape(query_rows, per_query).T,
        row_count,
    )

    if shards == 8:
        hold = lax.optimization_barrier
        far = swap(own, 4, shards)
        side = swap(own, 1, shards)
        near = swap(own, 2, shards)
        near_side = swap(own, 3, shards)
        decoded, rows = decode(pq_codes, codebook, full_rows)
        own_late, decoded = hold((own, decoded))
        far, decoded = hold((far, decoded))
        cross = swap(own_late, 7, shards)
        far_side = swap(far, 1, shards)
        far_near = swap(far, 2, shards)
        blocks = [own, side, near, near_side]
        found = exact(rows, blocks, groups, tops)
        scores = score_blocks(decoded, blocks, sub_width, per_query)
        far_side, far_near, cross, found, scores = hold(
            (far_side, far_near, cross, found, scores)
        )
        blocks = [far, far_side, far_near, cross]
        sent = exact(rows, blocks, groups, tops)
        approx_scores = late_approx(
            ids, lens, decoded, scores, blocks, list(range(8)), sub_width
        )
        kept = found + swap(sent, 4, shards)
        kept, approx_scores = hold((kept, approx_scores))
        parts = [kept[:, p * query_rows : (p + 1) * query_rows] for p in range(4)]
        total = parts[0]
        for distance in (1, 2, 3):
            total = total + swap(parts[distance], distance, shards)
    else:
        gathered = lax.all_gather(own, "corpus", axis=0)
        decoded, rows = decode(pq_codes, codebook, full_rows)
        answers, pieces = [], []
        step = 4
        for first in range(0, shards, step):
            blocks = [gathered[p] for p in range(first, first + step)]
            found = exact(rows, blocks, groups, tops)
            scores = score_blocks(decoded, blocks, sub_width, per_query)
            answers += [found[:, p * query_rows : (p + 1) * query_rows] for p in range(step)]
            some = slice(first, first + step)
            pieces.append(choose(ids[:, some], lens[some], scores))
        approx_scores = jnp.concatenate(pieces, axis=0)
        back = lax.all_to_all(jnp.stack(answers), "corpus", 0, 0, tiled=True)
        total = jnp.sum(back, axis=0)

    approx_scores = approx_scores.reshape(shards, 1, 1, slots, query_rows, B)
    return approx_scores, total.T.reshape(query_rows, groups, tops)


def solution(mesh):
    return jax.shard_map(
        local,
        mesh=mesh,
        in_specs=(
            P(("groups", "corpus", "replica"), None),
            P("groups", None),
            P(("groups", "corpus"), None),
            P(("groups", "corpus"), None),
            P("groups", "replica", "corpus", None),
            P("groups", "replica", "corpus"),
            P(("groups", "corpus", "replica"), None, None),
            P(("groups", "corpus", "replica"), None, None),
        ),
        out_specs=(
            P("groups", "replica", "corpus", None, None, None),
            P(("groups", "corpus", "replica"), None, None),
        ),
        check_vma=False,
    )
```

```python
import functools

import jax
import jax.numpy as jnp
from jax import lax
from jax.experimental import pallas as pl
from jax.experimental.pallas import tpu as pltpu
from jax.sharding import PartitionSpec as P

B = 256
NT = (((1,), (1,)), ((), ()))
IN_VMEM = pl.BlockSpec(memory_space=pltpu.VMEM)
IN_HBM = pl.BlockSpec(memory_space=pl.ANY)
IN_SMEM = pl.BlockSpec(memory_space=pltpu.SMEM)
EXACT_COST = 0
LIMIT = 24 * 2**20


def params():
    return pltpu.CompilerParams(vmem_limit_bytes=LIMIT)


def pick(table, index):
    dims = lax.GatherDimensionNumbers(
        offset_dims=(),
        collapsed_slice_dims=(0,),
        start_index_map=(0,),
        operand_batching_dims=(1,),
        start_indices_batching_dims=(1,),
    )
    return lax.gather(
        table,
        index[..., None],
        dims,
        slice_sizes=(1, 1),
        mode=lax.GatherScatterMode.PROMISE_IN_BOUNDS,
    )


def regroup_matrix(sub_width):
    run = 256 // sub_width
    source = lax.broadcasted_iota(jnp.int32, (256, 256), 0)
    target = lax.broadcasted_iota(jnp.int32, (256, 256), 1)
    return (source == (target % run) * sub_width + target // run).astype(jnp.bfloat16)


def pack_kernel(
    queries_ref, shard_ref, row_ref, out_ref, shard, row, sems, *, row_count
):
    query_rows, features = queries_ref.shape
    strips = features // 128
    copies = [
        pltpu.make_async_copy(shard_ref, shard, sems.at[strips]),
        pltpu.make_async_copy(row_ref, row, sems.at[strips + 1]),
    ]
    for strip in range(strips):
        copies.append(
            pltpu.make_async_copy(
                queries_ref.at[:, pl.ds(strip * 128, 128)],
                out_ref.at[pl.ds(strip * query_rows, query_rows)],
                sems.at[strip],
            )
        )
    for copy in copies:
        copy.start()
    copies[0].wait()
    copies[1].wait()
    place = shard[...] * (row_count // B) + row[...] // B
    tail = jnp.concatenate([place, row[...] % B], axis=1)
    out_ref[strips * query_rows :, :] = tail.astype(jnp.float32).astype(jnp.bfloat16)
    for copy in copies[2:]:
        copy.wait()


def pack(queries, cand_shard, cand_row, row_count):
    query_rows, features = queries.shape
    per_query = cand_row.shape[0]
    strips = features // 128
    return pl.pallas_call(
        functools.partial(pack_kernel, row_count=row_count),
        out_shape=pltpu.VMEM((strips * query_rows + per_query, 128), jnp.bfloat16),
        in_specs=[IN_HBM] * 3,
        out_specs=IN_VMEM,
        scratch_shapes=[
            pltpu.VMEM(cand_row.shape, jnp.int32),
            pltpu.VMEM(cand_row.shape, jnp.int32),
            pltpu.SemaphoreType.DMA((strips + 2,)),
        ],
        compiler_params=params(),
        cost_estimate=cost(0),
        name="pack",
    )(*map(in_hbm, (queries, cand_shard, cand_row)))


def decode_kernel(
    codes_ref, book_ref, rows_ref, out_ref, rows_out, codes, book, tables, sems, row_sems, *, step
):
    row_count, features = out_ref.shape
    centroids, code_count = book_ref.shape[0], codes_ref.shape[1]
    parts = row_count // step

    def fetch(part):
        here = pl.ds(pl.multiple_of(part * step, step), step)
        return pltpu.make_async_copy(codes_ref.at[here], codes.at[here], sems.at[part])

    book_copy = pltpu.make_async_copy(book_ref, book, sems.at[parts])
    book_copy.start()
    for part in range(parts):
        fetch(part).start()
    row_copies = []
    piece = row_count // row_sems.shape[0]
    for at in range(row_sems.shape[0]):
        here = pl.ds(at * piece, piece)
        row_copies.append(
            pltpu.make_async_copy(rows_ref.at[here], rows_out.at[here], row_sems.at[at])
        )
        row_copies[-1].start()
    regroup = regroup_matrix(features // code_count)
    book_copy.wait()
    for left in range(0, features, 256):
        tables[:, left : left + 256] = jnp.dot(
            book[:, left : left + 256], regroup, preferred_element_type=jnp.float32
        ).astype(jnp.bfloat16)

    @pl.loop(0, parts)
    def _(at):
        fetch(at).wait()
        here = pl.ds(pl.multiple_of(at * step, step), step)
        first = lax.broadcasted_iota(jnp.int32, (step, 128), 1) < 64
        for pair in range(code_count // 128):
            both = codes[here, pair * 128 : (pair + 1) * 128]
            turned = pltpu.roll(both, 64, 1)
            for side in range(2):
                index = jnp.where(first, both, turned) if side == 0 else jnp.where(first, turned, both)
                index = index.astype(jnp.int16)
                for half in range(2):
                    left = (pair * 2 + side) * 256 + half * 128
                    table = tables[:, left : left + 128]
                    pieces = [
                        pick(table, index[top : top + centroids])
                        for top in range(0, step, centroids)
                    ]
                    out_ref[here, left : left + 128] = jnp.concatenate(pieces, axis=0)

    for copy in row_copies:
        copy.wait()


def decode(pq_codes, codebook, full_rows):
    features = codebook.shape[1]
    rows = pq_codes.shape[0]
    step = 512
    return pl.pallas_call(
        functools.partial(decode_kernel, step=step),
        out_shape=[
            pltpu.VMEM((rows, features), jnp.bfloat16),
            pltpu.VMEM(full_rows.shape, full_rows.dtype),
        ],
        in_specs=[IN_HBM] * 3,
        out_specs=[IN_VMEM] * 2,
        scratch_shapes=[
            pltpu.VMEM(pq_codes.shape, jnp.int32),
            pltpu.VMEM(codebook.shape, codebook.dtype),
            pltpu.VMEM(codebook.shape, codebook.dtype),
            pltpu.SemaphoreType.DMA((rows // step + 1,)),
            pltpu.SemaphoreType.DMA((4,)),
        ],
        compiler_params=params(),
        cost_estimate=cost(0),
        name="decode",
    )(*map(in_hbm, (pq_codes, codebook, full_rows)))


def cost(size):
    return pl.CostEstimate(flops=size * 10**9, bytes_accessed=size * 2**20, transcendentals=0)


def in_hbm(x):
    return pltpu.with_memory_space_constraint(x, pltpu.HBM)


def in_vmem(x):
    return pltpu.with_memory_space_constraint(x, pltpu.VMEM)


def count_queries(block, rows, per_query):
    return (block.shape[0] - per_query) * 128 // rows.shape[1]


def fill(stack, blocks):
    query_rows = stack.shape[0] // len(blocks)
    for at, block in enumerate(blocks):
        for strip in range(stack.shape[1] // 128):
            stack[at * query_rows : (at + 1) * query_rows, strip * 128 : (strip + 1) * 128] = block[
                strip * query_rows : (strip + 1) * query_rows, :
            ]


def find(stack, rows_ref, blocks, per_query, groups):
    row_count = rows_ref.shape[0]
    width = stack.shape[0]
    query_rows = width // len(blocks)
    tops = per_query // groups
    scores = lax.dot_general(
        rows_ref[...], stack[...], NT, preferred_element_type=jnp.float32
    )
    tails = [block[-per_query:, :].astype(jnp.int32) for block in blocks]
    wanted = jnp.concatenate(
        [tail[:, :query_rows] * B + tail[:, query_rows : 2 * query_rows] for tail in tails], axis=1
    )
    wanted = wanted - lax.axis_index("corpus") * row_count
    mine = (wanted >= 0) & (wanted < row_count)
    kept = jnp.where(mine, wanted, -1)
    down = lax.broadcasted_iota(jnp.int32, (8, width), 0)
    found = []
    for group in range(groups):
        row = jnp.max(kept[group * tops : (group + 1) * tops], axis=0, keepdims=True)
        row = jnp.broadcast_to(row, (8, width)) - down
        total = jnp.zeros((8, width), jnp.float32)
        for top in range(0, row_count, 8):
            total = jnp.where(row == top, scores[top : top + 8], total)
        total = jnp.sum(total, axis=0, keepdims=True)
        found.append(jnp.broadcast_to(total, (tops, width)))
    return jnp.where(mine, jnp.concatenate(found, axis=0), 0.0)


def score(stack, decoded_ref, out_ref, sub_width):
    regroup = regroup_matrix(sub_width)
    for left in range(0, stack.shape[1], 256):
        run = slice(left, left + 256)
        stack[:, run] = jnp.dot(
            stack[:, run], regroup, preferred_element_type=jnp.float32
        ).astype(jnp.bfloat16)
    for block in range(out_ref.shape[0]):
        out_ref[block] = lax.dot_general(
            stack[...],
            decoded_ref[block * B : (block + 1) * B, :],
            NT,
            preferred_element_type=jnp.float32,
        ).astype(jnp.bfloat16)


def exact_kernel(rows_ref, *refs, per_query, groups):
    blocks, (found_ref, stack) = refs[:-2], refs[-2:]
    fill(stack, blocks)
    found_ref[...] = find(stack, rows_ref, blocks, per_query, groups)


def exact(full_rows, blocks, groups, tops):
    per_query = groups * tops
    width = len(blocks) * count_queries(blocks[0], full_rows, per_query)
    return pl.pallas_call(
        functools.partial(exact_kernel, per_query=per_query, groups=groups),
        out_shape=pltpu.VMEM((per_query, width), jnp.float32),
        in_specs=[IN_VMEM] * (1 + len(blocks)),
        out_specs=IN_VMEM,
        scratch_shapes=[pltpu.VMEM((width, full_rows.shape[1]), jnp.bfloat16)],
        compiler_params=params(),
        cost_estimate=cost(0),
        name="exact",
    )(*map(in_vmem, [full_rows] + blocks))


def scores_kernel(decoded_ref, *refs, sub_width):
    blocks, (scores_ref, stack) = refs[:-2], refs[-2:]
    fill(stack, blocks)
    score(stack, decoded_ref, scores_ref, sub_width)


def score_blocks(decoded, blocks, sub_width, per_query):
    width = len(blocks) * count_queries(blocks[0], decoded, per_query)
    rows, features = decoded.shape
    return pl.pallas_call(
        functools.partial(scores_kernel, sub_width=sub_width),
        out_shape=pltpu.VMEM((rows // B, width, B), jnp.bfloat16),
        in_specs=[IN_VMEM] * (1 + len(blocks)),
        out_specs=IN_VMEM,
        scratch_shapes=[pltpu.VMEM((width, features), jnp.bfloat16)],
        compiler_params=params(),
        cost_estimate=cost(0),
        name="score_blocks",
    )(*map(in_vmem, [decoded] + blocks))


def place_scores(ids_ref, len_ref, scores_ref, out_ref, owners):
    query_rows = out_ref.shape[2]
    for at, owner in enumerate(owners):
        here = slice(at * query_rows, (at + 1) * query_rows)
        for slot in range(out_ref.shape[1]):
            picked = scores_ref[ids_ref[slot, owner], here, :]
            out_ref[owner, slot] = jnp.where(slot < len_ref[owner], picked, jnp.zeros_like(picked))


def late_approx_kernel(
    ids_ref, len_ref, decoded_ref, scores_ref, *refs, places, sub_width
):
    blocks, (out_ref, stack, late_scores) = refs[:-3], refs[-3:]
    fill(stack, blocks)
    me = lax.axis_index("corpus")
    owners = [me ^ place for place in places]
    half = len(places) // 2
    place_scores(ids_ref, len_ref, scores_ref, out_ref, owners[:half])
    score(stack, decoded_ref, late_scores, sub_width)
    place_scores(ids_ref, len_ref, late_scores, out_ref, owners[half:])


def late_approx(probe_ids, probe_len, decoded, scores, blocks, places, sub_width):
    block_count, width, _ = scores.shape
    slots = probe_ids.shape[0]
    query_rows = width // len(blocks)
    return pl.pallas_call(
        functools.partial(late_approx_kernel, places=places, sub_width=sub_width),
        out_shape=pltpu.VMEM((len(places), slots, query_rows, B), jnp.bfloat16),
        in_specs=[IN_SMEM] * 2 + [IN_VMEM] * (2 + len(blocks)),
        out_specs=IN_VMEM,
        scratch_shapes=[
            pltpu.VMEM((width, decoded.shape[1]), jnp.bfloat16),
            pltpu.VMEM(scores.shape, jnp.bfloat16),
        ],
        compiler_params=params(),
        cost_estimate=cost(10),
        name="late_approx",
    )(probe_ids, probe_len, *map(in_vmem, [decoded, scores] + blocks))


def choose_kernel(ids_ref, len_ref, scores_ref, out_ref):
    place_scores(ids_ref, len_ref, scores_ref, out_ref, range(out_ref.shape[0]))


def choose(probe_ids, probe_len, scores):
    slots, count = probe_ids.shape
    query_rows = scores.shape[1] // count
    return pl.pallas_call(
        choose_kernel,
        out_shape=jax.ShapeDtypeStruct((count, slots, query_rows, B), jnp.bfloat16),
        in_specs=[IN_SMEM] * 2 + [IN_VMEM],
        out_specs=IN_VMEM,
        compiler_params=params(),
        name="choose",
    )(probe_ids, probe_len, scores)


def swap(x, distance, shards):
    return lax.ppermute(x, "corpus", [(i, i ^ distance) for i in range(shards)])


def local(queries, codebook, pq_codes, full_rows, probe_ids, probe_len, cand_shard, cand_row):
    shards = lax.axis_size("corpus")
    query_rows, features = queries.shape
    row_count = full_rows.shape[0]
    groups, tops = cand_shard.shape[1:]
    per_query = groups * tops
    slots = probe_ids.shape[-1]
    sub_width = features // pq_codes.shape[1]
    ids = probe_ids.reshape(shards, slots).T
    lens = probe_len.reshape(shards)
    own = pack(
        queries,
        cand_shard.reshape(query_rows, per_query).T,
        cand_row.reshape(query_rows, per_query).T,
        row_count,
    )

    if shards == 8:
        hold = lax.optimization_barrier
        far = swap(own, 4, shards)
        side = swap(own, 1, shards)
        near = swap(own, 2, shards)
        near_side = swap(own, 3, shards)
        decoded, rows = decode(pq_codes, codebook, full_rows)
        own_late, decoded = hold((own, decoded))
        far, decoded = hold((far, decoded))
        cross = swap(own_late, 7, shards)
        far_side = swap(far, 1, shards)
        far_near = swap(far, 2, shards)
        blocks = [own, near, side, near_side]
        found = exact(rows, blocks, groups, tops)
        scores = score_blocks(decoded, blocks, sub_width, per_query)
        far_side, far_near, cross, found, scores = hold(
            (far_side, far_near, cross, found, scores)
        )
        blocks = [far, far_near, far_side, cross]
        sent = exact(rows, blocks, groups, tops)
        approx_scores = late_approx(
            ids, lens, decoded, scores, blocks, [0, 2, 1, 3, 4, 6, 5, 7], sub_width
        )
        kept = found + swap(sent, 4, shards)
        kept, approx_scores = hold((kept, approx_scores))
        parts = [kept[:, p * query_rows : (p + 1) * query_rows] for p in range(4)]
        total = parts[0]
        for at, distance in [(3, 3), (2, 1), (1, 2)]:
            total = total + swap(parts[at], distance, shards)
    else:
        gathered = lax.all_gather(own, "corpus", axis=0)
        decoded, rows = decode(pq_codes, codebook, full_rows)
        answers, pieces = [], []
        step = 4
        for first in range(0, shards, step):
            blocks = [gathered[p] for p in range(first, first + step)]
            found = exact(rows, blocks, groups, tops)
            scores = score_blocks(decoded, blocks, sub_width, per_query)
            answers += [found[:, p * query_rows : (p + 1) * query_rows] for p in range(step)]
            some = slice(first, first + step)
            pieces.append(choose(ids[:, some], lens[some], scores))
        approx_scores = jnp.concatenate(pieces, axis=0)
        back = lax.all_to_all(jnp.stack(answers), "corpus", 0, 0, tiled=True)
        total = jnp.sum(back, axis=0)

    approx_scores = approx_scores.reshape(shards, 1, 1, slots, query_rows, B)
    return approx_scores, total.T.reshape(query_rows, groups, tops)


def solution(mesh):
    return jax.shard_map(
        local,
        mesh=mesh,
        in_specs=(
            P(("groups", "corpus", "replica"), None),
            P("groups", None),
            P(("groups", "corpus"), None),
            P(("groups", "corpus"), None),
            P("groups", "replica", "corpus", None),
            P("groups", "replica", "corpus"),
            P(("groups", "corpus", "replica"), None, None),
            P(("groups", "corpus", "replica"), None, None),
        ),
        out_specs=(
            P("groups", "replica", "corpus", None, None, None),
            P(("groups", "corpus", "replica"), None, None),
        ),
        check_vma=False,
    )
```
